32 devices in a mesh: row: 2 (over y), col: 4 (over z), rep: 4 (over x, core).
Axes of the slice: x: 2, y: 2, z: 4, core: 2. Of those that a mesh axis runs over, the one named last changes fastest.
Arguments:
- p_values: float32 [16, 4, 12, 128, 128], P(('row', 'col'), 'rep'), may hold values from -2.5 to 2.5
- p_cols: int32 [64, 12], replicated, may hold values from 0 to 63, as said below
- out_cols: int32 [64, 8], P(('row', 'col')), may hold values from 0 to 63, as said below
Outputs:
- square: float32 [64, 8, 128, 128], P(('row', 'col', 'rep'))
The draws below stay inside these ranges and needn't reach their ends.
Inputs may be any that keep to these rules, and one draw needn't show every extreme that they name: `p_cols`: block row r names 12 distinct block columns c with r - 16 <= c < r + 16; its slots l * 3 to (l + 1) * 3 - 1 hold exactly the 3 columns that are congruent to l modulo 4. `out_cols`: block row r names 8 distinct block columns c with r - 16 <= c <= r + 16.
All inputs are finite; a program needn't handle non-finite values.
Results may differ from the reference program's by a relative error of at most 0.0003.
Values sent between devices are 32-bit elements; how exact they have to be, the bound alone decides.
A program may use at most 64 MiB of HBM per device.

```python
import jax
import jax.numpy as jnp
from jax import lax

BS = 128
KL = 3
F = 8
LAYERS = 4
K = 12
NB = 64
W = 16


def draw_p_cols(key, part):
    groups = K // KL
    reach_count = 2 * W // groups
    row_ids = jnp.arange(NB, dtype=jnp.int32)[:, None, None]
    residue = jnp.arange(groups, dtype=jnp.int32)[None, :, None]
    steps_ahead = jnp.arange(reach_count, dtype=jnp.int32)[None, None, :]
    lowest = row_ids - W
    candidate = lowest + jnp.mod(residue - lowest, groups) + groups * steps_ahead
    inside = (candidate >= 0) & (candidate < NB)
    scores = jax.random.randint(jax.random.fold_in(key, 11), (NB, groups, reach_count), 0, 1 << 20, dtype=jnp.int32) * reach_count + steps_ahead
    boundary = (candidate == 0) | (candidate == NB - 1)
    scores = scores + jnp.where(boundary, 1 << 28, 0).astype(jnp.int32)
    scores = jnp.where(inside, scores, -1 - steps_ahead)
    ranked, chosen = lax.top_k(scores, KL)
    columns = jnp.take_along_axis(jnp.broadcast_to(candidate, scores.shape), chosen, axis=2)
    return columns.reshape(NB, K).astype(jnp.int32)


def draw_out_cols(key, part):
    span = 2 * W + 1
    row_ids = jnp.arange(NB, dtype=jnp.int32)[:, None]
    offsets = jnp.arange(span, dtype=jnp.int32)[None, :]
    candidate = row_ids - W + offsets
    inside = (candidate >= 0) & (candidate < NB)
    scores = jax.random.randint(jax.random.fold_in(key, 23), (NB, span), 0, 1 << 20, dtype=jnp.int32) * span + offsets
    boundary = (candidate == 0) | (candidate == NB - 1)
    scores = scores + jnp.where(boundary, 1 << 28, 0).astype(jnp.int32)
    scores = jnp.where(inside, scores, -1 - offsets)
    ranked, chosen = lax.top_k(scores, F)
    columns = jnp.take_along_axis(jnp.broadcast_to(candidate, scores.shape), chosen, axis=1)
    return columns.astype(jnp.int32)


def block_levels(own_key, dims, cuts, least, largest):
    def one(dim, parts):
        steps = jax.random.uniform(jax.random.fold_in(jax.random.fold_in(own_key, 6), dim), (parts,), jnp.float32, least / len(cuts), largest / len(cuts))
        return jnp.repeat(jnp.exp(steps), dims[dim] // parts).reshape((-1,) + (1,) * (len(dims) - dim - 1))

    level = one(*cuts[0])
    for cut in cuts[1:]:
        level = level * one(*cut)
    return level


def scatter_about(stream_key, dims, deviation, most, split=(), held_as=jnp.bfloat16):
    level = block_levels(stream_key, dims, split, -0.22, 0.18) if split else 1.0
    result = jax.random.normal(stream_key, dims, jnp.float32) * deviation * level
    return jnp.minimum(jnp.maximum(result, -most), most).astype(held_as)


def setup_inputs(seed: int = 0) -> dict:
    key_list = jax.random.split(jax.random.key(seed), 4)
    p_values = scatter_about(key_list[0], (NB // LAYERS, LAYERS, K, BS, BS), 0.18, 2.5, ((0, 8), (1, 4)), jnp.float32)
    p_cols = draw_p_cols(jax.random.fold_in(key_list[3], 71), 0)
    out_cols = draw_out_cols(jax.random.fold_in(key_list[3], 71), 0)
    return dict(p_values=p_values, p_cols=p_cols, out_cols=out_cols)


HIGHEST = lax.Precision.HIGHEST


def reference(p_values, p_cols, out_cols):
    stored = p_values.reshape(NB, K, BS, BS)
    slot_ids = jnp.arange(K, dtype=jnp.int32)

    def one_row(row_index):
        row_cols = p_cols[row_index]
        wanted = out_cols[row_index]
        far_cols = p_cols[row_cols]
        matches = far_cols[:, None, :] == wanted[None, :, None]
        slot_index = jnp.sum(jnp.where(matches, slot_ids[None, None, :], 0), axis=2).astype(jnp.int32)
        present = jnp.any(matches, axis=2)
        picked = stored[row_cols[:, None], slot_index]
        picked = jnp.where(present[:, :, None, None], picked, jnp.zeros_like(picked))
        return jnp.einsum("sab,sfbc->fac", stored[row_index], picked, precision=HIGHEST)

    return lax.map(one_row, jnp.arange(NB, dtype=jnp.int32))
```

```python
import jax
import jax.numpy as jnp
from jax import lax
from jax.experimental import pallas as pl
from jax.experimental.pallas import tpu as pltpu
from jax.sharding import PartitionSpec as P


def passed_along(x, axis, by):
    peers = lax.axis_size(axis)
    pairs = [(i, i + by) for i in range(peers) if 0 <= i + by < peers]
    return lax.ppermute(x, axis, pairs)


def two_part(x):
    high = x.astype(jnp.bfloat16)
    low = (x - high.astype(jnp.float32)).astype(jnp.bfloat16)
    return high, low


def products_kernel(table, entries_ref, window_ref, out_ref):
    row = pl.program_id(0)
    per_layer = entries_ref.shape[1]
    wanted = out_ref.shape[1]
    out_ref[...] = jnp.zeros_like(out_ref)
    for s in range(per_layer):
        a_high, a_low = two_part(entries_ref[0, s])

        def one_output(f, carry):
            where = table[(row * per_layer + s) * wanted + f]

            @pl.when(where >= 0)
            def _():
                b_high, b_low = two_part(window_ref[where])
                left = jnp.concatenate([a_high, a_low], axis=1)
                right = jnp.concatenate([b_high, b_high], axis=0)
                got = jnp.dot(left, right, preferred_element_type=jnp.float32)
                got += jnp.dot(a_high, b_low, preferred_element_type=jnp.float32)
                out_ref[0, f] += got

            return carry

        lax.fori_loop(0, wanted, one_output, 0, unroll=True)


def products(table, entries, window, wanted):
    rows, per_layer, order, _ = entries.shape
    return pl.pallas_call(
        products_kernel,
        out_shape=jax.ShapeDtypeStruct((rows, wanted, order, order), jnp.float32),
        grid_spec=pltpu.PrefetchScalarGridSpec(
            num_scalar_prefetch=1,
            grid=(rows,),
            in_specs=[
                pl.BlockSpec((1, per_layer, order, order), lambda r, t: (r, 0, 0, 0)),
                pl.BlockSpec(window.shape, lambda r, t: (0, 0, 0)),
            ],
            out_specs=pl.BlockSpec((1, wanted, order, order), lambda r, t: (r, 0, 0, 0)),
        ),
        compiler_params=pltpu.CompilerParams(vmem_limit_bytes=32 * 1024 * 1024),
        cost_estimate=pl.CostEstimate(
            flops=6 * rows * per_layer * wanted * order**3,
            bytes_accessed=4 * (window.size + entries.size + rows * wanted * order * order),
            transcendentals=0,
        ),
    )(table, entries, window)


def on_device(p_values, p_cols, out_cols):
    layers = lax.axis_size("rep")
    layer_index = lax.axis_index("rep")
    segment = lax.axis_index(("row", "col"))
    own_rows = p_values[:, 0]
    row_count, slot_total, order, _ = own_rows.shape
    per_layer = slot_total // layers
    seg_rows = row_count * layers
    wanted = out_cols.shape[1]
    ahead = passed_along(own_rows, ("row", "col"), 1)
    back = passed_along(own_rows, ("row", "col"), -1)
    ahead2 = passed_along(ahead, ("row", "col"), 1)
    back2 = passed_along(back, ("row", "col"), -1)
    gathered = lax.all_gather(p_values, "rep", axis=1, tiled=True)
    entries = lax.dynamic_slice_in_dim(gathered, layer_index * per_layer, per_layer, 2)
    entries = entries.reshape(seg_rows, per_layer, order, order)
    window = jnp.concatenate([ahead2, ahead, own_rows, back, back2], axis=0)
    window = window.reshape(-1, order, order)
    inner_cols = lax.dynamic_slice(
        p_cols, (segment * seg_rows, layer_index * per_layer), (seg_rows, per_layer)
    )
    far_cols = p_cols[inner_cols]
    slot_ids = jnp.arange(slot_total, dtype=jnp.int32)
    matches = far_cols[:, :, None, :] == out_cols[:, None, :, None]
    slot_index = jnp.max(jnp.where(matches, slot_ids, -1), axis=3)
    window_idx = inner_cols // layers - (segment - 2) * row_count
    table = jnp.where(slot_index >= 0, window_idx[:, :, None] * slot_total + slot_index, -1)
    shares = products(table.reshape(-1), entries, window, wanted)
    return lax.psum_scatter(shares, "rep", scatter_dimension=0, tiled=True)


def solution(mesh):
    in_specs = (P(("row", "col"), "rep", None, None, None), P(), P(("row", "col"), None))
    out_specs = P(("row", "col", "rep"), None, None, None)
    return jax.shard_map(
        on_device, mesh=mesh, in_specs=in_specs, out_specs=out_specs, check_vma=False
    )
```

```python
import functools

import jax
import jax.numpy as jnp
from jax import lax
from jax.experimental import pallas as pl
from jax.experimental.pallas import tpu as pltpu
from jax.sharding import PartitionSpec as P


CHUNKS = 4
MESH = pl.DeviceIdType.MESH


def window_kernel(
    rows, cols, own, win, transit, kept_sem, own_send, relay_send, transit_send, win_recv, transit_recv
):
    r, c = lax.axis_index("row"), lax.axis_index("col")
    last = cols - 1
    segment = r * cols + c
    size = own.shape[0] // CHUNKS
    at_edge = (c == 0) | (c == last)

    barrier = pltpu.get_barrier_semaphore()

    def greet(to_row, to_col):
        pl.semaphore_signal(
            barrier, inc=1, device_id={"row": to_row, "col": to_col}, device_id_type=MESH
        )

    greet(r, lax.rem(c + 1, cols))
    greet(r, lax.rem(c + cols - 1, cols))
    pl.when(at_edge & (r > 0))(lambda: greet(r - 1, c))
    pl.when(at_edge & (r < rows - 1))(lambda: greet(r + 1, c))
    peers = 2 + jnp.where(at_edge & (r > 0), 1, 0) + jnp.where(at_edge & (r < rows - 1), 1, 0)
    pl.semaphore_wait(barrier, peers)

    def part(k):
        return pl.ds(k * size, size)

    def slot(d, p):
        return (1 - p) if d == 0 else (3 + p)

    def step(d):
        return 1 if d == 0 else -1

    def in_range(at):
        return (at >= 0) & (at < rows * cols)

    def copy(source, target, sent, landed, to_row, to_col):
        return pltpu.make_async_remote_copy(
            src_ref=source,
            dst_ref=target,
            send_sem=sent,
            recv_sem=landed,
            device_id={"row": to_row, "col": to_col},
            device_id_type=MESH,
        )

    def outgoing(d, p, k):
        by = step(d)
        leaves = c == (last if d == 0 else 0)
        sends = in_range(segment + by)
        if p == 1:
            sends = sends & in_range(segment - by)
        source = own.at[part(k)] if p == 0 else win.at[slot(d, 0), part(k)]
        sent = own_send.at[d, k] if p == 0 else relay_send.at[d, k]
        near = copy(
            source, win.at[slot(d, p), part(k)], sent, win_recv.at[d, p, k], r, c + by
        )
        if k % 2 == 0:
            place = (r + by, c)
        else:
            place = (r, 0 if d == 0 else last)
        far = copy(
            source, transit.at[d, p, part(k)], sent, transit_recv.at[d, p, k], *place
        )
        return near, sends & jnp.logical_not(leaves), far, sends & leaves

    def passing(d, p, k):
        by = step(d)
        if k % 2 == 0:
            mine = (c == last) & (r > 0) if d == 0 else (c == 0) & (r < rows - 1)
            place = (r, 0 if d == 0 else last)
        else:
            mine = (c == 0) & (r < rows - 1) if d == 0 else (c == last) & (r > 0)
            place = (r + by, c)
        onward = copy(
            transit.at[d, p, part(k)],
            win.at[slot(d, p), part(k)],
            transit_send.at[d, p, k],
            win_recv.at[d, p, k],
            *place,
        )
        return onward, mine

    def landing(d, p, k):
        target = win.at[slot(d, p), part(k)]
        arrives = in_range(segment - (1 + p) * step(d))
        done = copy(target, target, own_send.at[d, k], win_recv.at[d, p, k], r, lax.rem(c + 1, cols))
        return done, arrives

    def send(d, p, k):
        near, near_on, far, far_on = outgoing(d, p, k)
        pl.when(near_on)(near.start)
        pl.when(far_on)(far.start)

    def pass_on(d, p, k):
        onward, mine = passing(d, p, k)

        @pl.when(mine)
        def _():
            held = transit.at[d, p, part(k)]
            copy(
                held, held, own_send.at[d, k], transit_recv.at[d, p, k], r, lax.rem(c + 1, cols)
            ).wait_recv()
            onward.start()

    def land(d, p, k):
        done, arrives = landing(d, p, k)
        pl.when(arrives)(done.wait_recv)

    for k in (1, 0, 3, 2):
        for d in range(2):
            send(d, 0, k)
    kept = pltpu.make_async_copy(own, win.at[2], kept_sem)
    kept.start()
    order = (1, 0, 3, 2)
    for i in range(CHUNKS + 1):
        if i < CHUNKS:
            for d in range(2):
                pass_on(d, 0, order[i])
            for d in range(2):
                land(d, 0, order[i])
                send(d, 1, order[i])
        if i > 0:
            for d in range(2):
                pass_on(d, 1, order[i - 1])
    for k in order:
        for d in range(2):
            land(d, 1, k)
    kept.wait()
    for k in range(CHUNKS):
        for d in range(2):
            for p in range(2):
                near, near_on, far, far_on = outgoing(d, p, k)
                pl.when(near_on)(near.wait_send)
                pl.when(far_on)(far.wait_send)
                onward, mine = passing(d, p, k)
                pl.when(mine)(onward.wait_send)


def gathered_window(own):
    rows, cols = lax.axis_size("row"), lax.axis_size("col")
    blocks, order, _ = own.shape
    dma = pltpu.SemaphoreType.DMA
    return pl.pallas_call(
        functools.partial(window_kernel, rows, cols),
        out_shape=jax.ShapeDtypeStruct((5, blocks, order, order), own.dtype),
        in_specs=[pl.BlockSpec(memory_space=pl.ANY)],
        out_specs=pl.BlockSpec(memory_space=pl.ANY),
        scratch_shapes=[
            pltpu.VMEM((2, 2, blocks, order, order), own.dtype),
            dma,
            dma((2, CHUNKS)),
            dma((2, CHUNKS)),
            dma((2, 2, CHUNKS)),
            dma((2, 2, CHUNKS)),
            dma((2, 2, CHUNKS)),
        ],
        compiler_params=pltpu.CompilerParams(
            collective_id=0, has_side_effects=True, vmem_limit_bytes=32 * 1024 * 1024
        ),
        cost_estimate=pl.CostEstimate(
            flops=0, bytes_accessed=16 * own.size * 5, transcendentals=0
        ),
    )(own)


def two_part(x):
    high = x.astype(jnp.bfloat16)
    low = (x - high.astype(jnp.float32)).astype(jnp.bfloat16)
    return high, low


def products_kernel(table, entries_ref, window_ref, out_ref):
    row = pl.program_id(0)
    per_layer = entries_ref.shape[1]
    wanted = out_ref.shape[1]
    out_ref[...] = jnp.zeros_like(out_ref)
    for s in range(per_layer):
        a_high, a_low = two_part(entries_ref[0, s])

        def one_output(f, carry):
            where = table[(row * per_layer + s) * wanted + f]

            @pl.when(where >= 0)
            def _():
                b_high, b_low = two_part(window_ref[where])
                left = jnp.concatenate([a_high, a_low], axis=1)
                right = jnp.concatenate([b_high, b_high], axis=0)
                got = jnp.dot(left, right, preferred_element_type=jnp.float32)
                got += jnp.dot(a_high, b_low, preferred_element_type=jnp.float32)
                out_ref[0, f] += got

            return carry

        lax.fori_loop(0, wanted, one_output, 0, unroll=True)


def products(table, entries, window, wanted):
    rows, per_layer, order, _ = entries.shape
    return pl.pallas_call(
        products_kernel,
        out_shape=jax.ShapeDtypeStruct((rows, wanted, order, order), jnp.float32),
        grid_spec=pltpu.PrefetchScalarGridSpec(
            num_scalar_prefetch=1,
            grid=(rows,),
            in_specs=[
                pl.BlockSpec((1, per_layer, order, order), lambda r, t: (r, 0, 0, 0)),
                pl.BlockSpec(window.shape, lambda r, t: (0, 0, 0)),
            ],
            out_specs=pl.BlockSpec((1, wanted, order, order), lambda r, t: (r, 0, 0, 0)),
        ),
        compiler_params=pltpu.CompilerParams(vmem_limit_bytes=32 * 1024 * 1024),
        cost_estimate=pl.CostEstimate(
            flops=6 * rows * per_layer * wanted * order**3,
            bytes_accessed=4 * (window.size + entries.size + rows * wanted * order * order),
            transcendentals=0,
        ),
    )(table, entries, window)


def on_device(p_values, p_cols, out_cols):
    layers = lax.axis_size("rep")
    layer_index = lax.axis_index("rep")
    segment = lax.axis_index(("row", "col"))
    own_rows = p_values[:, 0]
    row_count, slot_total, order, _ = own_rows.shape
    per_layer = slot_total // layers
    seg_rows = row_count * layers
    wanted = out_cols.shape[1]
    gathered = lax.all_gather(p_values, "rep", axis=1, tiled=True)
    entries = lax.dynamic_slice_in_dim(gathered, layer_index * per_layer, per_layer, 2)
    entries = entries.reshape(seg_rows, per_layer, order, order)
    window = gathered_window(own_rows.reshape(-1, order, order))
    window = window.reshape(-1, order, order)
    inner_cols = lax.dynamic_slice(
        p_cols, (segment * seg_rows, layer_index * per_layer), (seg_rows, per_layer)
    )
    far_cols = p_cols[inner_cols]
    slot_ids = jnp.arange(slot_total, dtype=jnp.int32)
    matches = far_cols[:, :, None, :] == out_cols[:, None, :, None]
    slot_index = jnp.max(jnp.where(matches, slot_ids, -1), axis=3)
    window_idx = inner_cols // layers - (segment - 2) * row_count
    table = jnp.where(slot_index >= 0, window_idx[:, :, None] * slot_total + slot_index, -1)
    shares = products(table.reshape(-1), entries, window, wanted)
    return lax.psum_scatter(shares, "rep", scatter_dimension=0, tiled=True)


def solution(mesh):
    in_specs = (P(("row", "col"), "rep", None, None, None), P(), P(("row", "col"), None))
    out_specs = P(("row", "col", "rep"), None, None, None)
    return jax.shard_map(
        on_device, mesh=mesh, in_specs=in_specs, out_specs=out_specs, check_vma=False
    )
```

```python
import functools

import jax
import jax.numpy as jnp
from jax import lax
from jax.experimental import pallas as pl
from jax.experimental.pallas import tpu as pltpu
from jax.sharding import PartitionSpec as P


CHUNKS = 4
MESH = pl.DeviceIdType.MESH


def window_kernel(
    rows, cols, own, win, transit, kept_sem, own_send, relay_send, transit_send, win_recv, transit_recv
):
    r, c = lax.axis_index("row"), lax.axis_index("col")
    last = cols - 1
    segment = r * cols + c
    size = own.shape[0] // CHUNKS
    at_edge = (c == 0) | (c == last)

    barrier = pltpu.get_barrier_semaphore()

    def greet(to_row, to_col):
        pl.semaphore_signal(
            barrier, inc=1, device_id={"row": to_row, "col": to_col}, device_id_type=MESH
        )

    greet(r, lax.rem(c + 1, cols))
    greet(r, lax.rem(c + cols - 1, cols))
    pl.when(at_edge & (r > 0))(lambda: greet(r - 1, c))
    pl.when(at_edge & (r < rows - 1))(lambda: greet(r + 1, c))
    peers = 2 + jnp.where(at_edge & (r > 0), 1, 0) + jnp.where(at_edge & (r < rows - 1), 1, 0)
    pl.semaphore_wait(barrier, peers)

    def part(k):
        return pl.ds(k * size, size)

    def slot(d, p):
        return (1 - p) if d == 0 else (3 + p)

    def step(d):
        return 1 if d == 0 else -1

    def in_range(at):
        return (at >= 0) & (at < rows * cols)

    def copy(source, target, sent, landed, to_row, to_col):
        return pltpu.make_async_remote_copy(
            src_ref=source,
            dst_ref=target,
            send_sem=sent,
            recv_sem=landed,
            device_id={"row": to_row, "col": to_col},
            device_id_type=MESH,
        )

    def outgoing(d, p, k):
        by = step(d)
        leaves = c == (last if d == 0 else 0)
        sends = in_range(segment + by)
        if p == 1:
            sends = sends & in_range(segment - by)
        source = own.at[part(k)] if p == 0 else win.at[slot(d, 0), part(k)]
        sent = own_send.at[d, k] if p == 0 else relay_send.at[d, k]
        near = copy(
            source, win.at[slot(d, p), part(k)], sent, win_recv.at[d, p, k], r, c + by
        )
        if k % 2 == 0:
            place = (r + by, c)
        else:
            place = (r, 0 if d == 0 else last)
        far = copy(
            source, transit.at[d, p, part(k)], sent, transit_recv.at[d, p, k], *place
        )
        return near, sends & jnp.logical_not(leaves), far, sends & leaves

    def passing(d, p, k):
        by = step(d)
        if k % 2 == 0:
            mine = (c == last) & (r > 0) if d == 0 else (c == 0) & (r < rows - 1)
            place = (r, 0 if d == 0 else last)
        else:
            mine = (c == 0) & (r < rows - 1) if d == 0 else (c == last) & (r > 0)
            place = (r + by, c)
        onward = copy(
            transit.at[d, p, part(k)],
            win.at[slot(d, p), part(k)],
            transit_send.at[d, p, k],
            win_recv.at[d, p, k],
            *place,
        )
        return onward, mine

    def landing(d, p, k):
        target = win.at[slot(d, p), part(k)]
        arrives = in_range(segment - (1 + p) * step(d))
        done = copy(target, target, own_send.at[d, k], win_recv.at[d, p, k], r, lax.rem(c + 1, cols))
        return done, arrives

    def send(d, p, k):
        near, near_on, far, far_on = outgoing(d, p, k)
        pl.when(near_on)(near.start)
        pl.when(far_on)(far.start)

    def pass_on(d, p, k):
        onward, mine = passing(d, p, k)

        @pl.when(mine)
        def _():
            held = transit.at[d, p, part(k)]
            copy(
                held, held, own_send.at[d, k], transit_recv.at[d, p, k], r, lax.rem(c + 1, cols)
            ).wait_recv()
            onward.start()

    def land(d, p, k):
        done, arrives = landing(d, p, k)
        pl.when(arrives)(done.wait_recv)

    for k in (1, 0, 3, 2):
        for d in range(2):
            send(d, 0, k)
    kept = pltpu.make_async_copy(own, win.at[2], kept_sem)
    kept.start()
    order = (1, 0, 3, 2)
    for i in range(CHUNKS + 1):
        if i < CHUNKS:
            for d in range(2):
                pass_on(d, 0, order[i])
            for d in range(2):
                land(d, 0, order[i])
                send(d, 1, order[i])
        if i > 0:
            for d in range(2):
                pass_on(d, 1, order[i - 1])
    for k in order:
        for d in range(2):
            land(d, 1, k)
    kept.wait()
    for k in range(CHUNKS):
        for d in range(2):
            for p in range(2):
                near, near_on, far, far_on = outgoing(d, p, k)
                pl.when(near_on)(near.wait_send)
                pl.when(far_on)(far.wait_send)
                onward, mine = passing(d, p, k)
                pl.when(mine)(onward.wait_send)


def gathered_window(own):
    rows, cols = lax.axis_size("row"), lax.axis_size("col")
    blocks, order, _ = own.shape
    dma = pltpu.SemaphoreType.DMA
    return pl.pallas_call(
        functools.partial(window_kernel, rows, cols),
        out_shape=jax.ShapeDtypeStruct((5, blocks, order, order), own.dtype),
        in_specs=[pl.BlockSpec(memory_space=pl.ANY)],
        out_specs=pl.BlockSpec(memory_space=pl.ANY),
        scratch_shapes=[
            pltpu.VMEM((2, 2, blocks, order, order), own.dtype),
            dma,
            dma((2, CHUNKS)),
            dma((2, CHUNKS)),
            dma((2, 2, CHUNKS)),
            dma((2, 2, CHUNKS)),
            dma((2, 2, CHUNKS)),
        ],
        compiler_params=pltpu.CompilerParams(
            collective_id=0, has_side_effects=True, vmem_limit_bytes=32 * 1024 * 1024
        ),
        cost_estimate=pl.CostEstimate(
            flops=0, bytes_accessed=16 * own.size * 5, transcendentals=0
        ),
    )(own)


def two_part(x):
    high = x.astype(jnp.bfloat16)
    low = (x - high.astype(jnp.float32)).astype(jnp.bfloat16)
    return high, low


def products_kernel(table, entries_ref, window_ref, out_ref):
    row = pl.program_id(0)
    per_layer = entries_ref.shape[1]
    wanted = out_ref.shape[1]
    out_ref[...] = jnp.zeros_like(out_ref)
    for s in range(per_layer):
        a_high, a_low = two_part(entries_ref[0, s])

        def one_output(f, carry):
            where = table[(row * per_layer + s) * wanted + f]

            @pl.when(where >= 0)
            def _():
                b_high, b_low = two_part(window_ref[where])
                left = jnp.concatenate([a_high, a_low], axis=1)
                right = jnp.concatenate([b_high, b_high], axis=0)
                got = jnp.dot(left, right, preferred_element_type=jnp.float32)
                got += jnp.dot(a_high, b_low, preferred_element_type=jnp.float32)
                out_ref[0, f] += got

            return carry

        lax.fori_loop(0, wanted, one_output, 0, unroll=True)


def products(table, entries, window, wanted):
    rows, per_layer, order, _ = entries.shape
    return pl.pallas_call(
        products_kernel,
        out_shape=jax.ShapeDtypeStruct((rows, wanted, order, order), jnp.float32),
        grid_spec=pltpu.PrefetchScalarGridSpec(
            num_scalar_prefetch=1,
            grid=(rows,),
            in_specs=[
                pl.BlockSpec((1, per_layer, order, order), lambda r, t: (r, 0, 0, 0)),
                pl.BlockSpec(window.shape, lambda r, t: (0, 0, 0)),
            ],
            out_specs=pl.BlockSpec((1, wanted, order, order), lambda r, t: (r, 0, 0, 0)),
        ),
        compiler_params=pltpu.CompilerParams(vmem_limit_bytes=32 * 1024 * 1024),
        cost_estimate=pl.CostEstimate(
            flops=6 * rows * per_layer * wanted * order**3,
            bytes_accessed=4 * (window.size + entries.size + rows * wanted * order * order),
            transcendentals=0,
        ),
    )(table, entries, window)


PIECES = 2


def share_sum_kernel(shares, out, from_twin, to_far, from_far, twin_send, twin_recv, far_send, far_recv):
    me = lax.axis_index("rep")
    twin = me + 1 - 2 * lax.rem(me, 2)
    far = lax.rem(me + 2, 4)
    far_twin = lax.rem(twin + 2, 4)
    rows = out.shape[0]
    size = out.shape[1] // PIECES

    barrier = pltpu.get_barrier_semaphore()
    for peer in (twin, far):
        pl.semaphore_signal(barrier, inc=1, device_id={"rep": peer}, device_id_type=MESH)
    pl.semaphore_wait(barrier, 2)

    pieces = [(q, i) for q in range(rows) for i in range(PIECES)]

    def twin_copy(h, q, i):
        owner = far_twin if h == 0 else twin
        return pltpu.make_async_remote_copy(
            src_ref=shares.at[owner * rows + q, pl.ds(i * size, size)],
            dst_ref=from_twin.at[h, q, pl.ds(i * size, size)],
            send_sem=twin_send.at[h, q, i],
            recv_sem=twin_recv.at[h, q, i],
            device_id={"rep": twin},
            device_id_type=MESH,
        )

    def far_copy(q, i):
        return pltpu.make_async_remote_copy(
            src_ref=to_far.at[q, pl.ds(i * size, size)],
            dst_ref=from_far.at[q, pl.ds(i * size, size)],
            send_sem=far_send.at[q, i],
            recv_sem=far_recv.at[q, i],
            device_id={"rep": far},
            device_id_type=MESH,
        )

    for h in range(2):
        for q, i in pieces:
            twin_copy(h, q, i).start()
    for q, i in pieces:
        part = pl.ds(i * size, size)
        twin_copy(0, q, i).wait_recv()
        to_far[q, part] = shares[far * rows + q, part] + from_twin[0, q, part]
        far_copy(q, i).start()
    for q, i in pieces:
        part = pl.ds(i * size, size)
        twin_copy(1, q, i).wait_recv()
        out[q, part] = shares[me * rows + q, part] + from_twin[1, q, part]
    for q, i in pieces:
        part = pl.ds(i * size, size)
        far_copy(q, i).wait_recv()
        out[q, part] = out[q, part] + from_far[q, part]
    for q, i in pieces:
        far_copy(q, i).wait_send()
        for h in range(2):
            twin_copy(h, q, i).wait_send()


def summed_shares(shares):
    assert lax.axis_size("rep") == 4
    kept = (shares.shape[0] // 4,) + shares.shape[1:]
    dma = pltpu.SemaphoreType.DMA
    return pl.pallas_call(
        share_sum_kernel,
        out_shape=jax.ShapeDtypeStruct(kept, shares.dtype),
        in_specs=[pl.BlockSpec(memory_space=pltpu.VMEM)],
        out_specs=pl.BlockSpec(memory_space=pltpu.VMEM),
        scratch_shapes=[
            pltpu.VMEM((2,) + kept, shares.dtype),
            pltpu.VMEM(kept, shares.dtype),
            pltpu.VMEM(kept, shares.dtype),
            dma((2, kept[0], PIECES)),
            dma((2, kept[0], PIECES)),
            dma((kept[0], PIECES)),
            dma((kept[0], PIECES)),
        ],
        compiler_params=pltpu.CompilerParams(
            collective_id=1, has_side_effects=True, vmem_limit_bytes=32 * 1024 * 1024
        ),
        cost_estimate=pl.CostEstimate(
            flops=shares.size, bytes_accessed=8 * shares.size, transcendentals=0
        ),
    )(shares)


def on_device(p_values, p_cols, out_cols):
    layers = lax.axis_size("rep")
    layer_index = lax.axis_index("rep")
    segment = lax.axis_index(("row", "col"))
    own_rows = p_values[:, 0]
    row_count, slot_total, order, _ = own_rows.shape
    per_layer = slot_total // layers
    seg_rows = row_count * layers
    wanted = out_cols.shape[1]
    gathered = lax.all_gather(p_values, "rep", axis=1, tiled=True)
    entries = lax.dynamic_slice_in_dim(gathered, layer_index * per_layer, per_layer, 2)
    entries = entries.reshape(seg_rows, per_layer, order, order)
    window = gathered_window(own_rows.reshape(-1, order, order))
    window = window.reshape(-1, order, order)
    inner_cols = lax.dynamic_slice(
        p_cols, (segment * seg_rows, layer_index * per_layer), (seg_rows, per_layer)
    )
    far_cols = p_cols[inner_cols]
    slot_ids = jnp.arange(slot_total, dtype=jnp.int32)
    matches = far_cols[:, :, None, :] == out_cols[:, None, :, None]
    slot_index = jnp.max(jnp.where(matches, slot_ids, -1), axis=3)
    window_idx = inner_cols // layers - (segment - 2) * row_count
    table = jnp.where(slot_index >= 0, window_idx[:, :, None] * slot_total + slot_index, -1)
    shares = products(table.reshape(-1), entries, window, wanted)
    return summed_shares(shares)


def solution(mesh):
    in_specs = (P(("row", "col"), "rep", None, None, None), P(), P(("row", "col"), None))
    out_specs = P(("row", "col", "rep"), None, None, None)
    return jax.shard_map(
        on_device, mesh=mesh, in_specs=in_specs, out_specs=out_specs, check_vma=False
    )
```

```python
import functools

import jax
import jax.numpy as jnp
from jax import lax
from jax.experimental import pallas as pl
from jax.experimental.pallas import tpu as pltpu
from jax.sharding import PartitionSpec as P


CHUNKS = 4
MESH = pl.DeviceIdType.MESH


def window_kernel(
    rows, cols, own, win, transit, kept_sem, own_send, relay_send, transit_send, win_recv, transit_recv
):
    r, c = lax.axis_index("row"), lax.axis_index("col")
    last = cols - 1
    segment = r * cols + c
    size = own.shape[0] // CHUNKS
    at_edge = (c == 0) | (c == last)

    barrier = pltpu.get_barrier_semaphore()

    def greet(to_row, to_col):
        pl.semaphore_signal(
            barrier, inc=1, device_id={"row": to_row, "col": to_col}, device_id_type=MESH
        )

    greet(r, lax.rem(c + 1, cols))
    greet(r, lax.rem(c + cols - 1, cols))
    pl.when(at_edge & (r > 0))(lambda: greet(r - 1, c))
    pl.when(at_edge & (r < rows - 1))(lambda: greet(r + 1, c))
    peers = 2 + jnp.where(at_edge & (r > 0), 1, 0) + jnp.where(at_edge & (r < rows - 1), 1, 0)
    pl.semaphore_wait(barrier, peers)

    def part(k):
        return pl.ds(k * size, size)

    def slot(d, p):
        return (1 - p) if d == 0 else (3 + p)

    def step(d):
        return 1 if d == 0 else -1

    def in_range(at):
        return (at >= 0) & (at < rows * cols)

    def copy(source, target, sent, landed, to_row, to_col):
        return pltpu.make_async_remote_copy(
            src_ref=source,
            dst_ref=target,
            send_sem=sent,
            recv_sem=landed,
            device_id={"row": to_row, "col": to_col},
            device_id_type=MESH,
        )

    def outgoing(d, p, k):
        by = step(d)
        leaves = c == (last if d == 0 else 0)
        sends = in_range(segment + by)
        if p == 1:
            sends = sends & in_range(segment - by)
        source = own.at[part(k)] if p == 0 else win.at[slot(d, 0), part(k)]
        sent = own_send.at[d, k] if p == 0 else relay_send.at[d, k]
        near = copy(
            source, win.at[slot(d, p), part(k)], sent, win_recv.at[d, p, k], r, c + by
        )
        if k % 2 == 0:
            place = (r + by, c)
        else:
            place = (r, 0 if d == 0 else last)
        far = copy(
            source, transit.at[d, p, part(k)], sent, transit_recv.at[d, p, k], *place
        )
        return near, sends & jnp.logical_not(leaves), far, sends & leaves

    def passing(d, p, k):
        by = step(d)
        if k % 2 == 0:
            mine = (c == last) & (r > 0) if d == 0 else (c == 0) & (r < rows - 1)
            place = (r, 0 if d == 0 else last)
        else:
            mine = (c == 0) & (r < rows - 1) if d == 0 else (c == last) & (r > 0)
            place = (r + by, c)
        onward = copy(
            transit.at[d, p, part(k)],
            win.at[slot(d, p), part(k)],
            transit_send.at[d, p, k],
            win_recv.at[d, p, k],
            *place,
        )
        return onward, mine

    def landing(d, p, k):
        target = win.at[slot(d, p), part(k)]
        arrives = in_range(segment - (1 + p) * step(d))
        done = copy(target, target, own_send.at[d, k], win_recv.at[d, p, k], r, lax.rem(c + 1, cols))
        return done, arrives

    def send(d, p, k):
        near, near_on, far, far_on = outgoing(d, p, k)
        pl.when(near_on)(near.start)
        pl.when(far_on)(far.start)

    def pass_on(d, p, k):
        onward, mine = passing(d, p, k)

        @pl.when(mine)
        def _():
            held = transit.at[d, p, part(k)]
            copy(
                held, held, own_send.at[d, k], transit_recv.at[d, p, k], r, lax.rem(c + 1, cols)
            ).wait_recv()
            onward.start()

    def land(d, p, k):
        done, arrives = landing(d, p, k)
        pl.when(arrives)(done.wait_recv)

    for k in (1, 0, 3, 2):
        for d in range(2):
            send(d, 0, k)
    kept = pltpu.make_async_copy(own, win.at[2], kept_sem)
    kept.start()
    order = (1, 0, 3, 2)
    for i in range(CHUNKS + 1):
        if i < CHUNKS:
            for d in range(2):
                pass_on(d, 0, order[i])
            for d in range(2):
                land(d, 0, order[i])
                send(d, 1, order[i])
        if i > 0:
            for d in range(2):
                pass_on(d, 1, order[i - 1])
    for k in order:
        for d in range(2):
            land(d, 1, k)
    kept.wait()
    for k in range(CHUNKS):
        for d in range(2):
            for p in range(2):
                near, near_on, far, far_on = outgoing(d, p, k)
                pl.when(near_on)(near.wait_send)
                pl.when(far_on)(far.wait_send)
                onward, mine = passing(d, p, k)
                pl.when(mine)(onward.wait_send)


def gathered_window(own):
    rows, cols = lax.axis_size("row"), lax.axis_size("col")
    blocks, order, _ = own.shape
    dma = pltpu.SemaphoreType.DMA
    return pl.pallas_call(
        functools.partial(window_kernel, rows, cols),
        out_shape=jax.ShapeDtypeStruct((5, blocks, order, order), own.dtype),
        in_specs=[pl.BlockSpec(memory_space=pl.ANY)],
        out_specs=pl.BlockSpec(memory_space=pl.ANY),
        scratch_shapes=[
            pltpu.VMEM((2, 2, blocks, order, order), own.dtype),
            dma,
            dma((2, CHUNKS)),
            dma((2, CHUNKS)),
            dma((2, 2, CHUNKS)),
            dma((2, 2, CHUNKS)),
            dma((2, 2, CHUNKS)),
        ],
        compiler_params=pltpu.CompilerParams(
            collective_id=0, has_side_effects=True, vmem_limit_bytes=32 * 1024 * 1024
        ),
        cost_estimate=pl.CostEstimate(
            flops=0, bytes_accessed=16 * own.size * 5, transcendentals=0
        ),
    )(own)


def two_part(x):
    high = x.astype(jnp.bfloat16)
    low = (x - high.astype(jnp.float32)).astype(jnp.bfloat16)
    return high, low


def products_kernel(table, entries_ref, window_ref, out_ref):
    row = pl.program_id(0)
    per_layer = entries_ref.shape[1]
    wanted, order = out_ref.shape[1], out_ref.shape[3]
    left = []
    for s in range(per_layer):
        a_high, a_low = two_part(entries_ref[0, s])
        left += [a_high, a_low, a_high]
    left = jnp.concatenate(left, axis=1)
    group = 2 if wanted % 2 == 0 else 1
    for first in range(0, wanted, group):
        columns = []
        for f in range(first, first + group):
            right = []
            for s in range(per_layer):
                where = table[(row * per_layer + s) * wanted + f]
                block = window_ref[jnp.maximum(where, 0)]
                block = jnp.where(where >= 0, block, jnp.zeros_like(block))
                b_high, b_low = two_part(block)
                right += [b_high, b_high, b_low]
            columns.append(jnp.concatenate(right, axis=0))
        got = jnp.dot(
            left, jnp.concatenate(columns, axis=1), preferred_element_type=jnp.float32
        )
        for at in range(group):
            out_ref[0, first + at] = got[:, at * order : (at + 1) * order]


def products(table, entries, window, wanted):
    rows, per_layer, order, _ = entries.shape
    return pl.pallas_call(
        products_kernel,
        out_shape=jax.ShapeDtypeStruct((rows, wanted, order, order), jnp.float32),
        grid_spec=pltpu.PrefetchScalarGridSpec(
            num_scalar_prefetch=1,
            grid=(rows,),
            in_specs=[
                pl.BlockSpec((1, per_layer, order, order), lambda r, t: (r, 0, 0, 0)),
                pl.BlockSpec(window.shape, lambda r, t: (0, 0, 0)),
            ],
            out_specs=pl.BlockSpec((1, wanted, order, order), lambda r, t: (r, 0, 0, 0)),
        ),
        compiler_params=pltpu.CompilerParams(vmem_limit_bytes=32 * 1024 * 1024),
        cost_estimate=pl.CostEstimate(
            flops=6 * rows * per_layer * wanted * order**3,
            bytes_accessed=4 * (window.size + entries.size + rows * wanted * order * order),
            transcendentals=0,
        ),
    )(table, entries, window)


PIECES = 2


def share_sum_kernel(shares, out, from_twin, to_far, from_far, twin_send, twin_recv, far_send, far_recv):
    me = lax.axis_index("rep")
    twin = me + 1 - 2 * lax.rem(me, 2)
    far = lax.rem(me + 2, 4)
    far_twin = lax.rem(twin + 2, 4)
    rows = out.shape[0]
    size = out.shape[1] // PIECES

    barrier = pltpu.get_barrier_semaphore()
    for peer in (twin, far):
        pl.semaphore_signal(barrier, inc=1, device_id={"rep": peer}, device_id_type=MESH)
    pl.semaphore_wait(barrier, 2)

    pieces = [(q, i) for q in range(rows) for i in range(PIECES)]

    def twin_copy(h, q, i):
        owner = far_twin if h == 0 else twin
        return pltpu.make_async_remote_copy(
            src_ref=shares.at[owner * rows + q, pl.ds(i * size, size)],
            dst_ref=from_twin.at[h, q, pl.ds(i * size, size)],
            send_sem=twin_send.at[h, q, i],
            recv_sem=twin_recv.at[h, q, i],
            device_id={"rep": twin},
            device_id_type=MESH,
        )

    def far_copy(q, i):
        return pltpu.make_async_remote_copy(
            src_ref=to_far.at[q, pl.ds(i * size, size)],
            dst_ref=from_far.at[q, pl.ds(i * size, size)],
            send_sem=far_send.at[q, i],
            recv_sem=far_recv.at[q, i],
            device_id={"rep": far},
            device_id_type=MESH,
        )

    for h in range(2):
        for q, i in pieces:
            twin_copy(h, q, i).start()
    for q, i in pieces:
        part = pl.ds(i * size, size)
        twin_copy(0, q, i).wait_recv()
        to_far[q, part] = shares[far * rows + q, part] + from_twin[0, q, part]
        far_copy(q, i).start()
    for q, i in pieces:
        part = pl.ds(i * size, size)
        twin_copy(1, q, i).wait_recv()
        out[q, part] = shares[me * rows + q, part] + from_twin[1, q, part]
    for q, i in pieces:
        part = pl.ds(i * size, size)
        far_copy(q, i).wait_recv()
        out[q, part] = out[q, part] + from_far[q, part]
    for q, i in pieces:
        far_copy(q, i).wait_send()
        for h in range(2):
            twin_copy(h, q, i).wait_send()


def summed_shares(shares):
    assert lax.axis_size("rep") == 4
    kept = (shares.shape[0] // 4,) + shares.shape[1:]
    dma = pltpu.SemaphoreType.DMA
    return pl.pallas_call(
        share_sum_kernel,
        out_shape=jax.ShapeDtypeStruct(kept, shares.dtype),
        in_specs=[pl.BlockSpec(memory_space=pltpu.VMEM)],
        out_specs=pl.BlockSpec(memory_space=pltpu.VMEM),
        scratch_shapes=[
            pltpu.VMEM((2,) + kept, shares.dtype),
            pltpu.VMEM(kept, shares.dtype),
            pltpu.VMEM(kept, shares.dtype),
            dma((2, kept[0], PIECES)),
            dma((2, kept[0], PIECES)),
            dma((kept[0], PIECES)),
            dma((kept[0], PIECES)),
        ],
        compiler_params=pltpu.CompilerParams(
            collective_id=1, has_side_effects=True, vmem_limit_bytes=32 * 1024 * 1024
        ),
        cost_estimate=pl.CostEstimate(
            flops=shares.size, bytes_accessed=8 * shares.size, transcendentals=0
        ),
    )(shares)


def on_device(p_values, p_cols, out_cols):
    layers = lax.axis_size("rep")
    layer_index = lax.axis_index("rep")
    segment = lax.axis_index(("row", "col"))
    own_rows = p_values[:, 0]
    row_count, slot_total, order, _ = own_rows.shape
    per_layer = slot_total // layers
    seg_rows = row_count * layers
    wanted = out_cols.shape[1]
    gathered = lax.all_gather(p_values, "rep", axis=1, tiled=True)
    entries = lax.dynamic_slice_in_dim(gathered, layer_index * per_layer, per_layer, 2)
    entries = entries.reshape(seg_rows, per_layer, order, order)
    window = gathered_window(own_rows.reshape(-1, order, order))
    window = window.reshape(-1, order, order)
    inner_cols = lax.dynamic_slice(
        p_cols, (segment * seg_rows, layer_index * per_layer), (seg_rows, per_layer)
    )
    far_cols = p_cols[inner_cols]
    slot_ids = jnp.arange(slot_total, dtype=jnp.int32)
    matches = far_cols[:, :, None, :] == out_cols[:, None, :, None]
    slot_index = jnp.max(jnp.where(matches, slot_ids, -1), axis=3)
    window_idx = inner_cols // layers - (segment - 2) * row_count
    table = jnp.where(slot_index >= 0, window_idx[:, :, None] * slot_total + slot_index, -1)
    shares = products(table.reshape(-1), entries, window, wanted)
    return summed_shares(shares)


def solution(mesh):
    in_specs = (P(("row", "col"), "rep", None, None, None), P(), P(("row", "col"), None))
    out_specs = P(("row", "col", "rep"), None, None, None)
    return jax.shard_map(
        on_device, mesh=mesh, in_specs=in_specs, out_specs=out_specs, check_vma=False
    )
```

```python
import functools

import jax
import jax.numpy as jnp
from jax import lax
from jax.experimental import pallas as pl
from jax.experimental.pallas import tpu as pltpu
from jax.sharding import PartitionSpec as P


CHUNKS = 8
MESH = pl.DeviceIdType.MESH


def window_kernel(
    rows, cols, own, win, transit, kept_sem, own_send, relay_send, transit_send, win_recv, transit_recv
):
    r, c = lax.axis_index("row"), lax.axis_index("col")
    last = cols - 1
    segment = r * cols + c
    size = own.shape[0] // CHUNKS
    at_edge = (c == 0) | (c == last)

    barrier = pltpu.get_barrier_semaphore()

    def greet(to_row, to_col):
        pl.semaphore_signal(
            barrier, inc=1, device_id={"row": to_row, "col": to_col}, device_id_type=MESH
        )

    greet(r, lax.rem(c + 1, cols))
    greet(r, lax.rem(c + cols - 1, cols))
    pl.when(at_edge & (r > 0))(lambda: greet(r - 1, c))
    pl.when(at_edge & (r < rows - 1))(lambda: greet(r + 1, c))
    peers = 2 + jnp.where(at_edge & (r > 0), 1, 0) + jnp.where(at_edge & (r < rows - 1), 1, 0)
    pl.semaphore_wait(barrier, peers)

    def part(k):
        return pl.ds(k * size, size)

    def slot(d, p):
        return (1 - p) if d == 0 else (3 + p)

    def step(d):
        return 1 if d == 0 else -1

    def in_range(at):
        return (at >= 0) & (at < rows * cols)

    def copy(source, target, sent, landed, to_row, to_col):
        return pltpu.make_async_remote_copy(
            src_ref=source,
            dst_ref=target,
            send_sem=sent,
            recv_sem=landed,
            device_id={"row": to_row, "col": to_col},
            device_id_type=MESH,
        )

    def outgoing(d, p, k):
        by = step(d)
        leaves = c == (last if d == 0 else 0)
        sends = in_range(segment + by)
        if p == 1:
            sends = sends & in_range(segment - by)
        source = own.at[part(k)] if p == 0 else win.at[slot(d, 0), part(k)]
        sent = own_send.at[d, k] if p == 0 else relay_send.at[d, k]
        near = copy(
            source, win.at[slot(d, p), part(k)], sent, win_recv.at[d, p, k], r, c + by
        )
        if k % 2 == 0:
            place = (r + by, c)
        else:
            place = (r, 0 if d == 0 else last)
        far = copy(
            source, transit.at[d, p, part(k)], sent, transit_recv.at[d, p, k], *place
        )
        return near, sends & jnp.logical_not(leaves), far, sends & leaves

    def passing(d, p, k):
        by = step(d)
        if k % 2 == 0:
            mine = (c == last) & (r > 0) if d == 0 else (c == 0) & (r < rows - 1)
            place = (r, 0 if d == 0 else last)
        else:
            mine = (c == 0) & (r < rows - 1) if d == 0 else (c == last) & (r > 0)
            place = (r + by, c)
        onward = copy(
            transit.at[d, p, part(k)],
            win.at[slot(d, p), part(k)],
            transit_send.at[d, p, k],
            win_recv.at[d, p, k],
            *place,
        )
        return onward, mine

    def landing(d, p, k):
        target = win.at[slot(d, p), part(k)]
        arrives = in_range(segment - (1 + p) * step(d))
        done = copy(target, target, own_send.at[d, k], win_recv.at[d, p, k], r, lax.rem(c + 1, cols))
        return done, arrives

    def send(d, p, k):
        near, near_on, far, far_on = outgoing(d, p, k)
        pl.when(near_on)(near.start)
        pl.when(far_on)(far.start)

    def pass_on(d, p, k):
        onward, mine = passing(d, p, k)

        @pl.when(mine)
        def _():
            held = transit.at[d, p, part(k)]
            copy(
                held, held, own_send.at[d, k], transit_recv.at[d, p, k], r, lax.rem(c + 1, cols)
            ).wait_recv()
            onward.start()

    def land(d, p, k):
        done, arrives = landing(d, p, k)
        pl.when(arrives)(done.wait_recv)

    order = [k + 1 - 2 * (k % 2) for k in range(CHUNKS)]
    for k in order:
        for d in range(2):
            send(d, 0, k)
    kept = pltpu.make_async_copy(own, win.at[2], kept_sem)
    kept.start()
    for i in range(CHUNKS + 1):
        if i < CHUNKS:
            for d in range(2):
                pass_on(d, 0, order[i])
            for d in range(2):
                land(d, 0, order[i])
                send(d, 1, order[i])
        if i > 0:
            for d in range(2):
                pass_on(d, 1, order[i - 1])
    for k in order:
        for d in range(2):
            land(d, 1, k)
    kept.wait()
    for k in range(CHUNKS):
        for d in range(2):
            for p in range(2):
                near, near_on, far, far_on = outgoing(d, p, k)
                pl.when(near_on)(near.wait_send)
                pl.when(far_on)(far.wait_send)
                onward, mine = passing(d, p, k)
                pl.when(mine)(onward.wait_send)


def gathered_window(own):
    rows, cols = lax.axis_size("row"), lax.axis_size("col")
    blocks, order, _ = own.shape
    dma = pltpu.SemaphoreType.DMA
    return pl.pallas_call(
        functools.partial(window_kernel, rows, cols),
        out_shape=jax.ShapeDtypeStruct((5, blocks, order, order), own.dtype),
        in_specs=[pl.BlockSpec(memory_space=pl.ANY)],
        out_specs=pl.BlockSpec(memory_space=pl.ANY),
        scratch_shapes=[
            pltpu.VMEM((2, 2, blocks, order, order), own.dtype),
            dma,
            dma((2, CHUNKS)),
            dma((2, CHUNKS)),
            dma((2, 2, CHUNKS)),
            dma((2, 2, CHUNKS)),
            dma((2, 2, CHUNKS)),
        ],
        compiler_params=pltpu.CompilerParams(
            collective_id=0, has_side_effects=True, vmem_limit_bytes=32 * 1024 * 1024
        ),
        cost_estimate=pl.CostEstimate(
            flops=0, bytes_accessed=16 * own.size * 5, transcendentals=0
        ),
    )(own)


def two_part(x):
    high = x.astype(jnp.bfloat16)
    low = (x - high.astype(jnp.float32)).astype(jnp.bfloat16)
    return high, low


def products_kernel(table, entries_ref, window_ref, out_ref):
    row = pl.program_id(0)
    per_layer = entries_ref.shape[1]
    wanted, order = out_ref.shape[1], out_ref.shape[3]
    left = []
    for s in range(per_layer):
        a_high, a_low = two_part(entries_ref[0, s])
        left += [a_high, a_low, a_high]
    left = jnp.concatenate(left, axis=1)
    group = 2 if wanted % 2 == 0 else 1
    for first in range(0, wanted, group):
        columns = []
        for f in range(first, first + group):
            right = []
            for s in range(per_layer):
                where = table[(row * per_layer + s) * wanted + f]
                block = window_ref[jnp.maximum(where, 0)]
                block = jnp.where(where >= 0, block, jnp.zeros_like(block))
                b_high, b_low = two_part(block)
                right += [b_high, b_high, b_low]
            columns.append(jnp.concatenate(right, axis=0))
        got = jnp.dot(
            left, jnp.concatenate(columns, axis=1), preferred_element_type=jnp.float32
        )
        for at in range(group):
            out_ref[0, first + at] = got[:, at * order : (at + 1) * order]


def products(table, entries, window, wanted):
    rows, per_layer, order, _ = entries.shape
    return pl.pallas_call(
        products_kernel,
        out_shape=jax.ShapeDtypeStruct((rows, wanted, order, order), jnp.float32),
        grid_spec=pltpu.PrefetchScalarGridSpec(
            num_scalar_prefetch=1,
            grid=(rows,),
            in_specs=[
                pl.BlockSpec((1, per_layer, order, order), lambda r, t: (r, 0, 0, 0)),
                pl.BlockSpec(window.shape, lambda r, t: (0, 0, 0)),
            ],
            out_specs=pl.BlockSpec((1, wanted, order, order), lambda r, t: (r, 0, 0, 0)),
        ),
        compiler_params=pltpu.CompilerParams(vmem_limit_bytes=32 * 1024 * 1024),
        cost_estimate=pl.CostEstimate(
            flops=6 * rows * per_layer * wanted * order**3,
            bytes_accessed=4 * (window.size + entries.size + rows * wanted * order * order),
            transcendentals=0,
        ),
    )(table, entries, window)


PIECES = 2


def share_sum_kernel(shares, out, from_twin, to_far, from_far, twin_send, twin_recv, far_send, far_recv):
    me = lax.axis_index("rep")
    twin = me + 1 - 2 * lax.rem(me, 2)
    far = lax.rem(me + 2, 4)
    far_twin = lax.rem(twin + 2, 4)
    rows = out.shape[0]
    size = out.shape[1] // PIECES

    barrier = pltpu.get_barrier_semaphore()
    for peer in (twin, far):
        pl.semaphore_signal(barrier, inc=1, device_id={"rep": peer}, device_id_type=MESH)
    pl.semaphore_wait(barrier, 2)

    pieces = [(q, i) for q in range(rows) for i in range(PIECES)]

    def twin_copy(h, q, i):
        owner = far_twin if h == 0 else twin
        return pltpu.make_async_remote_copy(
            src_ref=shares.at[owner * rows + q, pl.ds(i * size, size)],
            dst_ref=from_twin.at[h, q, pl.ds(i * size, size)],
            send_sem=twin_send.at[h, q, i],
            recv_sem=twin_recv.at[h, q, i],
            device_id={"rep": twin},
            device_id_type=MESH,
        )

    def far_copy(q, i):
        return pltpu.make_async_remote_copy(
            src_ref=to_far.at[q, pl.ds(i * size, size)],
            dst_ref=from_far.at[q, pl.ds(i * size, size)],
            send_sem=far_send.at[q, i],
            recv_sem=far_recv.at[q, i],
            device_id={"rep": far},
            device_id_type=MESH,
        )

    for h in range(2):
        for q, i in pieces:
            twin_copy(h, q, i).start()
    for q, i in pieces:
        part = pl.ds(i * size, size)
        twin_copy(0, q, i).wait_recv()
        to_far[q, part] = shares[far * rows + q, part] + from_twin[0, q, part]
        far_copy(q, i).start()
    for q, i in pieces:
        part = pl.ds(i * size, size)
        twin_copy(1, q, i).wait_recv()
        out[q, part] = shares[me * rows + q, part] + from_twin[1, q, part]
    for q, i in pieces:
        part = pl.ds(i * size, size)
        far_copy(q, i).wait_recv()
        out[q, part] = out[q, part] + from_far[q, part]
    for q, i in pieces:
        far_copy(q, i).wait_send()
        for h in range(2):
            twin_copy(h, q, i).wait_send()


def summed_shares(shares):
    assert lax.axis_size("rep") == 4
    kept = (shares.shape[0] // 4,) + shares.shape[1:]
    dma = pltpu.SemaphoreType.DMA
    return pl.pallas_call(
        share_sum_kernel,
        out_shape=jax.ShapeDtypeStruct(kept, shares.dtype),
        in_specs=[pl.BlockSpec(memory_space=pltpu.VMEM)],
        out_specs=pl.BlockSpec(memory_space=pltpu.VMEM),
        scratch_shapes=[
            pltpu.VMEM((2,) + kept, shares.dtype),
            pltpu.VMEM(kept, shares.dtype),
            pltpu.VMEM(kept, shares.dtype),
            dma((2, kept[0], PIECES)),
            dma((2, kept[0], PIECES)),
            dma((kept[0], PIECES)),
            dma((kept[0], PIECES)),
        ],
        compiler_params=pltpu.CompilerParams(
            collective_id=1, has_side_effects=True, vmem_limit_bytes=32 * 1024 * 1024
        ),
        cost_estimate=pl.CostEstimate(
            flops=shares.size, bytes_accessed=8 * shares.size, transcendentals=0
        ),
    )(shares)


def on_device(p_values, p_cols, out_cols):
    layers = lax.axis_size("rep")
    layer_index = lax.axis_index("rep")
    segment = lax.axis_index(("row", "col"))
    own_rows = p_values[:, 0]
    row_count, slot_total, order, _ = own_rows.shape
    per_layer = slot_total // layers
    seg_rows = row_count * layers
    wanted = out_cols.shape[1]
    gathered = lax.all_gather(p_values, "rep", axis=1, tiled=True)
    entries = lax.dynamic_slice_in_dim(gathered, layer_index * per_layer, per_layer, 2)
    entries = entries.reshape(seg_rows, per_layer, order, order)
    window = gathered_window(own_rows.reshape(-1, order, order))
    window = window.reshape(-1, order, order)
    inner_cols = lax.dynamic_slice(
        p_cols, (segment * seg_rows, layer_index * per_layer), (seg_rows, per_layer)
    )
    far_cols = p_cols[inner_cols]
    slot_ids = jnp.arange(slot_total, dtype=jnp.int32)
    matches = far_cols[:, :, None, :] == out_cols[:, None, :, None]
    slot_index = jnp.max(jnp.where(matches, slot_ids, -1), axis=3)
    window_idx = inner_cols // layers - (segment - 2) * row_count
    table = jnp.where(slot_index >= 0, window_idx[:, :, None] * slot_total + slot_index, -1)
    shares = products(table.reshape(-1), entries, window, wanted)
    return summed_shares(shares)


def solution(mesh):
    in_specs = (P(("row", "col"), "rep", None, None, None), P(), P(("row", "col"), None))
    out_specs = P(("row", "col", "rep"), None, None, None)
    return jax.shard_map(
        on_device, mesh=mesh, in_specs=in_specs, out_specs=out_specs, check_vma=False
    )
```

```python
import functools

import jax
import jax.numpy as jnp
from jax import lax
from jax.experimental import pallas as pl
from jax.experimental.pallas import tpu as pltpu
from jax.sharding import PartitionSpec as P


CHUNKS = 4
MESH = pl.DeviceIdType.MESH


def window_kernel(
    rows, cols, own, win, transit, kept_sem, own_send, relay_send, transit_send, win_recv, transit_recv
):
    r, c = lax.axis_index("row"), lax.axis_index("col")
    last = cols - 1
    segment = r * cols + c
    size = own.shape[0] // CHUNKS
    at_edge = (c == 0) | (c == last)

    barrier = pltpu.get_barrier_semaphore()

    def greet(to_row, to_col):
        pl.semaphore_signal(
            barrier, inc=1, device_id={"row": to_row, "col": to_col}, device_id_type=MESH
        )

    greet(r, lax.rem(c + 1, cols))
    greet(r, lax.rem(c + cols - 1, cols))
    pl.when(at_edge & (r > 0))(lambda: greet(r - 1, c))
    pl.when(at_edge & (r < rows - 1))(lambda: greet(r + 1, c))
    peers = 2 + jnp.where(at_edge & (r > 0), 1, 0) + jnp.where(at_edge & (r < rows - 1), 1, 0)
    pl.semaphore_wait(barrier, peers)

    def part(k):
        return pl.ds(k * size, size)

    def slot(d, p):
        return (1 - p) if d == 0 else (3 + p)

    def step(d):
        return 1 if d == 0 else -1

    def in_range(at):
        return (at >= 0) & (at < rows * cols)

    def copy(source, target, sent, landed, to_row, to_col):
        return pltpu.make_async_remote_copy(
            src_ref=source,
            dst_ref=target,
            send_sem=sent,
            recv_sem=landed,
            device_id={"row": to_row, "col": to_col},
            device_id_type=MESH,
        )

    def outgoing(d, p, k):
        by = step(d)
        leaves = c == (last if d == 0 else 0)
        sends = in_range(segment + by)
        if p == 1:
            sends = sends & in_range(segment - by)
        source = own.at[part(k)] if p == 0 else win.at[slot(d, 0), part(k)]
        sent = own_send.at[d, k] if p == 0 else relay_send.at[d, k]
        near = copy(
            source, win.at[slot(d, p), part(k)], sent, win_recv.at[d, p, k], r, c + by
        )
        if k % 2 == 0:
            place = (r + by, c)
        else:
            place = (r, 0 if d == 0 else last)
        far = copy(
            source, transit.at[d, p, part(k)], sent, transit_recv.at[d, p, k], *place
        )
        return near, sends & jnp.logical_not(leaves), far, sends & leaves

    def passing(d, p, k):
        by = step(d)
        if k % 2 == 0:
            mine = (c == last) & (r > 0) if d == 0 else (c == 0) & (r < rows - 1)
            place = (r, 0 if d == 0 else last)
        else:
            mine = (c == 0) & (r < rows - 1) if d == 0 else (c == last) & (r > 0)
            place = (r + by, c)
        onward = copy(
            transit.at[d, p, part(k)],
            win.at[slot(d, p), part(k)],
            transit_send.at[d, p, k],
            win_recv.at[d, p, k],
            *place,
        )
        return onward, mine

    def landing(d, p, k):
        target = win.at[slot(d, p), part(k)]
        arrives = in_range(segment - (1 + p) * step(d))
        done = copy(target, target, own_send.at[d, k], win_recv.at[d, p, k], r, lax.rem(c + 1, cols))
        return done, arrives

    def send(d, p, k):
        near, near_on, far, far_on = outgoing(d, p, k)
        pl.when(near_on)(near.start)
        pl.when(far_on)(far.start)

    def pass_on(d, p, k):
        onward, mine = passing(d, p, k)

        @pl.when(mine)
        def _():
            held = transit.at[d, p, part(k)]
            copy(
                held, held, own_send.at[d, k], transit_recv.at[d, p, k], r, lax.rem(c + 1, cols)
            ).wait_recv()
            onward.start()

    def land(d, p, k):
        done, arrives = landing(d, p, k)
        pl.when(arrives)(done.wait_recv)

    for k in (1, 0, 3, 2):
        for d in range(2):
            send(d, 0, k)
    kept = pltpu.make_async_copy(own, win.at[2], kept_sem)
    kept.start()
    order = (1, 0, 3, 2)
    for i in range(CHUNKS + 1):
        if i < CHUNKS:
            for d in range(2):
                pass_on(d, 0, order[i])
            for d in range(2):
                land(d, 0, order[i])
                send(d, 1, order[i])
        if i > 0:
            for d in range(2):
                pass_on(d, 1, order[i - 1])
    for k in order:
        for d in range(2):
            land(d, 1, k)
    kept.wait()
    for k in range(CHUNKS):
        for d in range(2):
            for p in range(2):
                near, near_on, far, far_on = outgoing(d, p, k)
                pl.when(near_on)(near.wait_send)
                pl.when(far_on)(far.wait_send)
                onward, mine = passing(d, p, k)
                pl.when(mine)(onward.wait_send)


def gathered_window(own):
    rows, cols = lax.axis_size("row"), lax.axis_size("col")
    blocks, order, _ = own.shape
    dma = pltpu.SemaphoreType.DMA
    return pl.pallas_call(
        functools.partial(window_kernel, rows, cols),
        out_shape=jax.ShapeDtypeStruct((5, blocks, order, order), own.dtype),
        in_specs=[pl.BlockSpec(memory_space=pl.ANY)],
        out_specs=pl.BlockSpec(memory_space=pl.ANY),
        scratch_shapes=[
            pltpu.VMEM((2, 2, blocks, order, order), own.dtype),
            dma,
            dma((2, CHUNKS)),
            dma((2, CHUNKS)),
            dma((2, 2, CHUNKS)),
            dma((2, 2, CHUNKS)),
            dma((2, 2, CHUNKS)),
        ],
        compiler_params=pltpu.CompilerParams(
            collective_id=0, has_side_effects=True, vmem_limit_bytes=32 * 1024 * 1024
        ),
        cost_estimate=pl.CostEstimate(
            flops=0, bytes_accessed=16 * own.size * 5, transcendentals=0
        ),
    )(own)


def two_part(x):
    high = x.astype(jnp.bfloat16)
    low = (x - high.astype(jnp.float32)).astype(jnp.bfloat16)
    return high, low


def products_kernel(table, layer, entries_ref, window_ref, out_ref):
    row = pl.program_id(0)
    per_layer = entries_ref.shape[2]
    wanted, order = out_ref.shape[1], out_ref.shape[3]
    left = []
    for s in range(per_layer):
        a_high, a_low = two_part(entries_ref[0, 0, s])
        left += [a_high, a_low, a_high]
    left = jnp.concatenate(left, axis=1)
    group = 2 if wanted % 2 == 0 else 1
    for first in range(0, wanted, group):
        columns = []
        for f in range(first, first + group):
            right = []
            for s in range(per_layer):
                where = table[(row * per_layer + s) * wanted + f]
                block = window_ref[jnp.maximum(where, 0)]
                block = jnp.where(where >= 0, block, jnp.zeros_like(block))
                b_high, b_low = two_part(block)
                right += [b_high, b_high, b_low]
            columns.append(jnp.concatenate(right, axis=0))
        got = jnp.dot(
            left, jnp.concatenate(columns, axis=1), preferred_element_type=jnp.float32
        )
        for at in range(group):
            out_ref[0, first + at] = got[:, at * order : (at + 1) * order]


def products(table, layer, gathered, window, wanted):
    row_count, layers, slot_total, order, _ = gathered.shape
    rows, per_layer = row_count * layers, slot_total // layers
    return pl.pallas_call(
        products_kernel,
        out_shape=jax.ShapeDtypeStruct((rows, wanted, order, order), jnp.float32),
        grid_spec=pltpu.PrefetchScalarGridSpec(
            num_scalar_prefetch=2,
            grid=(rows,),
            in_specs=[
                pl.BlockSpec(
                    (1, 1, per_layer, order, order),
                    lambda r, t, m: (r // layers, r % layers, m[0], 0, 0),
                ),
                pl.BlockSpec(window.shape, lambda r, t, m: (0, 0, 0)),
            ],
            out_specs=pl.BlockSpec((1, wanted, order, order), lambda r, t, m: (r, 0, 0, 0)),
        ),
        compiler_params=pltpu.CompilerParams(vmem_limit_bytes=32 * 1024 * 1024),
        cost_estimate=pl.CostEstimate(
            flops=6 * rows * per_layer * wanted * order**3,
            bytes_accessed=4 * (window.size + gathered.size // layers + rows * wanted * order * order),
            transcendentals=0,
        ),
    )(table, layer, gathered, window)


PIECES = 2


def share_sum_kernel(shares, out, from_twin, to_far, from_far, twin_send, twin_recv, far_send, far_recv):
    me = lax.axis_index("rep")
    twin = me + 1 - 2 * lax.rem(me, 2)
    far = lax.rem(me + 2, 4)
    far_twin = lax.rem(twin + 2, 4)
    rows = out.shape[0]
    size = out.shape[1] // PIECES

    barrier = pltpu.get_barrier_semaphore()
    for peer in (twin, far):
        pl.semaphore_signal(barrier, inc=1, device_id={"rep": peer}, device_id_type=MESH)
    pl.semaphore_wait(barrier, 2)

    pieces = [(q, i) for q in range(rows) for i in range(PIECES)]

    def twin_copy(h, q, i):
        owner = far_twin if h == 0 else twin
        return pltpu.make_async_remote_copy(
            src_ref=shares.at[owner * rows + q, pl.ds(i * size, size)],
            dst_ref=from_twin.at[h, q, pl.ds(i * size, size)],
            send_sem=twin_send.at[h, q, i],
            recv_sem=twin_recv.at[h, q, i],
            device_id={"rep": twin},
            device_id_type=MESH,
        )

    def far_copy(q, i):
        return pltpu.make_async_remote_copy(
            src_ref=to_far.at[q, pl.ds(i * size, size)],
            dst_ref=from_far.at[q, pl.ds(i * size, size)],
            send_sem=far_send.at[q, i],
            recv_sem=far_recv.at[q, i],
            device_id={"rep": far},
            device_id_type=MESH,
        )

    for h in range(2):
        for q, i in pieces:
            twin_copy(h, q, i).start()
    for q, i in pieces:
        part = pl.ds(i * size, size)
        twin_copy(0, q, i).wait_recv()
        to_far[q, part] = shares[far * rows + q, part] + from_twin[0, q, part]
        far_copy(q, i).start()
    for q, i in pieces:
        part = pl.ds(i * size, size)
        twin_copy(1, q, i).wait_recv()
        out[q, part] = shares[me * rows + q, part] + from_twin[1, q, part]
    for q, i in pieces:
        part = pl.ds(i * size, size)
        far_copy(q, i).wait_recv()
        out[q, part] = out[q, part] + from_far[q, part]
    for q, i in pieces:
        far_copy(q, i).wait_send()
        for h in range(2):
            twin_copy(h, q, i).wait_send()


def summed_shares(shares):
    assert lax.axis_size("rep") == 4
    kept = (shares.shape[0] // 4,) + shares.shape[1:]
    dma = pltpu.SemaphoreType.DMA
    return pl.pallas_call(
        share_sum_kernel,
        out_shape=jax.ShapeDtypeStruct(kept, shares.dtype),
        in_specs=[pl.BlockSpec(memory_space=pltpu.VMEM)],
        out_specs=pl.BlockSpec(memory_space=pltpu.VMEM),
        scratch_shapes=[
            pltpu.VMEM((2,) + kept, shares.dtype),
            pltpu.VMEM(kept, shares.dtype),
            pltpu.VMEM(kept, shares.dtype),
            dma((2, kept[0], PIECES)),
            dma((2, kept[0], PIECES)),
            dma((kept[0], PIECES)),
            dma((kept[0], PIECES)),
        ],
        compiler_params=pltpu.CompilerParams(
            collective_id=1, has_side_effects=True, vmem_limit_bytes=32 * 1024 * 1024
        ),
        cost_estimate=pl.CostEstimate(
            flops=shares.size, bytes_accessed=8 * shares.size, transcendentals=0
        ),
    )(shares)


def on_device(p_values, p_cols, out_cols):
    layers = lax.axis_size("rep")
    layer_index = lax.axis_index("rep")
    segment = lax.axis_index(("row", "col"))
    own_rows = p_values[:, 0]
    row_count, slot_total, order, _ = own_rows.shape
    per_layer = slot_total // layers
    seg_rows = row_count * layers
    wanted = out_cols.shape[1]
    gathered = lax.all_gather(p_values, "rep", axis=1, tiled=True)
    window = gathered_window(own_rows.reshape(-1, order, order))
    window = window.reshape(-1, order, order)
    inner_cols = lax.dynamic_slice(
        p_cols, (segment * seg_rows, layer_index * per_layer), (seg_rows, per_layer)
    )
    far_cols = p_cols[inner_cols]
    slot_ids = jnp.arange(slot_total, dtype=jnp.int32)
    matches = far_cols[:, :, None, :] == out_cols[:, None, :, None]
    slot_index = jnp.max(jnp.where(matches, slot_ids, -1), axis=3)
    window_idx = inner_cols // layers - (segment - 2) * row_count
    table = jnp.where(slot_index >= 0, window_idx[:, :, None] * slot_total + slot_index, -1)
    shares = products(table.reshape(-1), layer_index.astype(jnp.int32)[None], gathered, window, wanted)
    return summed_shares(shares)


def solution(mesh):
    in_specs = (P(("row", "col"), "rep", None, None, None), P(), P(("row", "col"), None))
    out_specs = P(("row", "col", "rep"), None, None, None)
    return jax.shard_map(
        on_device, mesh=mesh, in_specs=in_specs, out_specs=out_specs, check_vma=False
    )
```
